512 devices in a mesh: island: 4 (over y_hi, core), fsdp: 32 (over y_lo, z), tp: 4 (over x).
Axes of the slice: x: 4, y: 4 (y_hi: 2, y_lo: 2; y = y_hi * 2 + y_lo), z: 16, core: 2. Of those that a mesh axis runs over, the one named last changes fastest.
Arguments:
- weights: bfloat16 [4, 6144, 4096], P('island', 'fsdp', 'tp'), may hold values from -6 to 6
- grads: bfloat16 [4, 6144, 4096], P('island', 'fsdp', 'tp'), may hold values from -200 to 200
- first_moment: bfloat16 [4, 6144, 4096], P('island', 'fsdp', 'tp'), may hold values from -3 to 3
- second_moment: bfloat16 [4, 6144, 4096], P('island', 'fsdp', 'tp'), may hold values from 0.049804688 to 0.5
- bases: bfloat16 [4, 4, 4096, 4096], P('island', None, 'tp', 'fsdp'), may hold values from -0.09375 to 0.09375
- outer_delta: bfloat16 [4, 6144, 4096], P('island', 'fsdp', 'tp'), may hold values from -3 to 3
- outer_momentum: bfloat16 [6144, 4096], P('fsdp', 'tp'), may hold values from -3 to 3
- row_fragment: int32 [6144], P('fsdp'), may hold values from 0 to 3
- sync_fragment: int32 [1], replicated, may hold values from 0 to 3
- block_map: int32 [4], P('island'), may hold values from 0 to 3
Outputs:
- new_weights: bfloat16 [4, 6144, 4096], P('island', 'fsdp', 'tp')
- new_first: bfloat16 [4, 6144, 4096], P('island', 'fsdp', 'tp')
- new_second: bfloat16 [4, 6144, 4096], P('island', 'fsdp', 'tp')
- new_momentum: bfloat16 [6144, 4096], P('fsdp', 'tp')
The draws below stay inside these ranges and needn't reach their ends.
All inputs are finite; a program needn't handle non-finite values.
Results may differ from the reference program's by a relative error of at most 0.0049.
Values may be sent and summed in bfloat16 or wider, within the bound.
No kernel may reach another device: no remote copies, remote signals or barrier semaphores. Data moves between devices by JAX's collectives and lax.ppermute only.
A program may use at most 64 MiB of HBM per device.

```python
import math
import jax
import jax.numpy as jnp
from jax import lax

K = 4096
N = 6144
NB = 4
FRAGS = 4
ISL = 4


def replica_levels(key_order):
    order = jax.random.permutation(key_order, ISL).astype(jnp.float32)
    half = ISL // 2
    low_span = max(half - 1, 1)
    high_span = max(ISL - half - 1, 1)
    low_level = 0.12 + 0.13 * order / low_span
    high_level = 1.5 * jnp.exp(jnp.log(jnp.float32(3.3)) * (order - half) / high_span)
    return jnp.where(order < half, low_level, high_level).reshape(ISL, 1, 1)


def draw_grads(key, part):
    key = jax.random.fold_in(key, 11)
    key_base = jax.random.fold_in(key, 0)
    key_rows = jax.random.fold_in(key, 1)
    key_cols = jax.random.fold_in(key, 2)
    key_order = jax.random.fold_in(key, 4)
    row_pos = (jnp.arange(N, dtype=jnp.float32) / N).reshape(1, N, 1)
    col_pos = (jnp.arange(K, dtype=jnp.float32) / K).reshape(1, 1, K)
    row_rand = jax.random.uniform(key_rows, (ISL, N, 1), jnp.float32)
    col_rand = jax.random.uniform(key_cols, (ISL, 1, K), jnp.float32)
    spread = jnp.log(jnp.float32(10.0))
    values = jnp.clip(jax.random.normal(key_base, (ISL, N, K), jnp.float32), -6.0, 6.0)
    base_rms = jnp.square((jnp.exp(spread) - 1.0) / spread)
    factor = replica_levels(key_order) / base_rms
    row_scale = jnp.exp(spread * (0.5 * row_pos + 0.5 * row_rand))
    col_scale = jnp.exp(spread * (0.5 * col_pos + 0.5 * col_rand))
    return (factor * row_scale * col_scale * values).astype(jnp.bfloat16)


def touch_ends(result, stream_key, smallest, largest):
    longest = result.shape.index(max(result.shape))
    spots = []
    for shift in (0, 1):
        where = [jax.random.randint(jax.random.fold_in(stream_key, axis), (), 0, length) for axis, length in enumerate(result.shape)]
        where[longest] = (where[longest] + shift) % result.shape[longest]
        spots.append(tuple(where))
    return result.at[spots[0]].set(smallest).at[spots[1]].set(largest)


def level_of(rng, shape, cuts, least, top_value):
    loudness, own = 1.0, jax.random.fold_in(rng, 6)
    for axis_at, parts in cuts:
        heights = jnp.exp(jax.random.uniform(jax.random.fold_in(own, axis_at), (parts,), jnp.float32, least / len(cuts), top_value / len(cuts)))
        loudness = loudness * jnp.repeat(heights, shape[axis_at] // parts).reshape([-1 if axis == axis_at else 1 for axis in range(len(shape))])
    return loudness


def scatter_about(stream_key, dims, deviation, bound, cuts=(), kind=jnp.bfloat16):
    factor_of = level_of(stream_key, dims, cuts, -0.22, 0.18) if cuts else 1.0
    drawn = jax.random.normal(stream_key, dims, jnp.float32) * deviation * factor_of
    return jnp.minimum(jnp.maximum(drawn, -bound), bound).astype(kind)


def setup_inputs(seed: int = 0) -> dict:
    arg_keys = jax.random.split(jax.random.key(seed), 11)
    return {
        "weights": scatter_about(arg_keys[0], (ISL, N, K), 1.0, 6.0, ((0, 4), (1, 32), (2, 4))),
        "grads": draw_grads(jax.random.fold_in(arg_keys[10], 71), 0),
        "first_moment": scatter_about(arg_keys[2], (ISL, N, K), 0.3, 3.0, ((0, 4), (1, 32), (2, 4))),
        "second_moment": jnp.clip(jnp.exp(math.log(0.5) - 2.306499 * jax.random.uniform(arg_keys[3], (ISL, N, K), jnp.float32) ** level_of(arg_keys[3], (ISL, N, K), ((0, 4), (1, 32), (2, 4)), -0.2, 0.2)), 0.049804688, 0.5).astype(jnp.bfloat16),
        "bases": scatter_about(arg_keys[4], (ISL, NB, K, K), K ** -0.5, 0.09375, ((0, 4), (2, 4), (3, 32))),
        "outer_delta": scatter_about(arg_keys[5], (ISL, N, K), 0.3, 3.0, ((0, 4), (1, 32), (2, 4))),
        "outer_momentum": scatter_about(arg_keys[6], (N, K), 0.3, 3.0, ((0, 32), (1, 4))),
        "row_fragment": touch_ends(jax.random.randint(arg_keys[7], (N,), 0, FRAGS), jax.random.fold_in(arg_keys[7], 1), 0, FRAGS - 1).astype(jnp.int32),
        "sync_fragment": jax.random.randint(arg_keys[8], (1,), 0, FRAGS).astype(jnp.int32),
        "block_map": touch_ends(jax.random.randint(arg_keys[9], (ISL,), 0, NB), jax.random.fold_in(arg_keys[9], 1), 0, NB - 1).astype(jnp.int32),
    }


beta_first = 0.9
beta_second = 0.95
adam_epsilon = 1e-08
inner_rate = 0.3
outer_rate = 0.7
nesterov = 0.9
clip_ratio = 0.5

def reference(weights, grads, first_moment, second_moment, bases, outer_delta, outer_momentum, row_fragment, sync_fragment, block_map):
    delta_mean = lax.optimization_barrier(jnp.sum(outer_delta.astype(jnp.float32), axis=0)) / ISL
    synced = (row_fragment == sync_fragment[0])[:, None]
    momentum = outer_momentum.astype(jnp.float32)
    momentum = jnp.where(synced, nesterov * momentum + delta_mean, momentum)
    correction = jnp.where(synced, outer_rate * (nesterov * momentum + delta_mean), jnp.float32(0.0))
    limit = clip_ratio * jnp.sqrt(jnp.float32(N * K))

    def one_replica(items):
        weight, grad, first, second, blocks, which = items
        basis = lax.dynamic_index_in_dim(blocks, which.astype(jnp.int32), 0, keepdims=False)
        squares = jnp.sum(jnp.square(grad.astype(jnp.float32)))
        clip = jnp.minimum(jnp.float32(1.0), limit / jnp.sqrt(squares + 1e-06))
        rotated = jnp.dot(grad, basis, preferred_element_type=jnp.float32)
        scaled = clip * rotated
        first_new = beta_first * first.astype(jnp.float32) + (1.0 - beta_first) * scaled
        second_new = beta_second * second.astype(jnp.float32) + (1.0 - beta_second) * scaled * scaled
        direction = (first_new / (jnp.sqrt(second_new) + adam_epsilon)).astype(jnp.bfloat16)
        update = jnp.dot(direction, basis.T, preferred_element_type=jnp.float32)
        weight_new = weight.astype(jnp.float32) - inner_rate * update - correction
        return (weight_new.astype(jnp.bfloat16), first_new.astype(jnp.bfloat16), second_new.astype(jnp.bfloat16))
    new_weights, new_first, new_second = lax.map(one_replica, (weights, grads, first_moment, second_moment, bases, block_map))
    return (new_weights, new_first, new_second, momentum.astype(jnp.bfloat16))
```

```python
import jax
import jax.numpy as jnp
import numpy as np
from jax import lax
from jax.experimental import pallas as pl
from jax.experimental.pallas import tpu as pltpu
from jax.sharding import PartitionSpec as P

K = 4096
N = 6144

beta_first = 0.9
beta_second = 0.95
adam_epsilon = 1e-08
inner_rate = 0.3
outer_rate = 0.7
nesterov = 0.9
clip_ratio = 0.5

ZS = 16
YS = 2
XS = 4
PLANE = YS * XS
BOTH = ("fsdp", "tp")
PLANE_GROUPS = [[(y * ZS + z) * XS + x for y in range(YS) for x in range(XS)] for z in range(ZS)]
Z_GROUPS = [[y * ZS + z for z in range(ZS)] for y in range(YS)]
Y_SWAP = [(f, (f + ZS) % (YS * ZS)) for f in range(YS * ZS)]


def x_shift(s):
    return [(x, (x + s) % XS) for x in range(XS)]


def plane_exchange(value):
    return lax.all_to_all(
        value, BOTH, split_axis=0, concat_axis=0, axis_index_groups=PLANE_GROUPS, tiled=True
    )


def total_squares(grad):
    total = jnp.full((8, 128), jnp.sum(jnp.square(grad.astype(jnp.float32))))
    for bit in (1, 2):
        total = total + lax.ppermute(total, "tp", [(x, x ^ bit) for x in range(XS)])
    for bit in (1, 2, 4, 8, 16):
        total = total + lax.ppermute(total, "fsdp", [(f, f ^ bit) for f in range(YS * ZS)])
    return total[0, 0]


def swap_matrix():
    row = lax.broadcasted_iota(jnp.int32, (1024, 1024), 0)
    col = lax.broadcasted_iota(jnp.int32, (1024, 1024), 1)
    swapped = (col // 16 % 8) * 128 + (col // 128) * 16 + col % 16
    return (row == swapped).astype(jnp.bfloat16)


def core_kernel(where_ref, clip_ref, a0, a1, a2, a3, b_ref, m_ref, rot_ref, upd_ref, dir_ref):
    y = where_ref[0]
    x = where_ref[1]
    clip = clip_ref[0]
    pieces = (a0, a1, a2, a3)
    for u in range(YS):
        row = lax.rem(y + u, YS)
        acc = jnp.zeros((192, 512), jnp.float32)
        for s in range(XS):
            at = pl.multiple_of(lax.rem(x + XS - s, XS) * 1024, 1024)
            acc = acc + lax.dot_general(
                pieces[s][u],
                b_ref[:, pl.ds(at, 1024)],
                (((1,), (1,)), ((), ())),
                preferred_element_type=jnp.float32,
            )
        for t in range(XS):
            rotated = acc[:, t * 128 : (t + 1) * 128]
            rot_ref[row * XS + t] = rotated.astype(jnp.bfloat16)
            scaled = clip * rotated
            first = beta_first * m_ref[row * XS + t, 0].astype(jnp.float32) + (1.0 - beta_first) * scaled
            second = (
                beta_second * m_ref[row * XS + t, 1].astype(jnp.float32)
                + (1.0 - beta_second) * scaled * scaled
            )
            dir_ref[:, t * 128 : (t + 1) * 128] = (
                first / (jnp.sqrt(second) + adam_epsilon)
            ).astype(jnp.bfloat16)
        for t in range(XS):
            upd_ref[row * XS + t] = jnp.dot(
                dir_ref[...], b_ref[:, t * 1024 : (t + 1) * 1024], preferred_element_type=jnp.float32
            ).astype(jnp.bfloat16)


def core(where, clip, pieces, basis, moments):
    vmem = pl.BlockSpec(memory_space=pltpu.VMEM)
    smem = pl.BlockSpec(memory_space=pltpu.SMEM)
    return pl.pallas_call(
        core_kernel,
        out_shape=(
            jax.ShapeDtypeStruct((PLANE, 192, 128), jnp.bfloat16),
            jax.ShapeDtypeStruct((PLANE, 192, 1024), jnp.bfloat16),
        ),
        in_specs=[smem, smem] + [vmem] * 6,
        out_specs=(vmem, vmem),
        scratch_shapes=[pltpu.VMEM((192, 512), jnp.bfloat16)],
        compiler_params=pltpu.CompilerParams(vmem_limit_bytes=48 * 2**20),
        cost_estimate=pl.CostEstimate(
            flops=4 * 384 * 4096 * 512, bytes_accessed=11 * 2**20, transcendentals=384 * 512
        ),
    )(where, clip, *pieces, basis, moments)


def on_device(
    weights,
    grads,
    first_moment,
    second_moment,
    bases,
    outer_delta,
    outer_momentum,
    row_fragment,
    sync_fragment,
    block_map,
):
    chosen = lax.dynamic_index_in_dim(bases[0], block_map[0], 0, keepdims=False)
    mixed = plane_exchange(chosen.T)
    mixed = mixed.reshape(YS, XS, 16, 1024).transpose(0, 2, 1, 3).reshape(YS, 16, K)
    basis = lax.all_gather(mixed, "fsdp", axis=1, axis_index_groups=Z_GROUPS, tiled=True)
    basis = basis.reshape(512, K)
    mixed, grad, first, second, delta = lax.optimization_barrier(
        (mixed, grads[0], first_moment[0], second_moment[0], outer_delta[0])
    )

    y_index = lax.axis_index("fsdp") // ZS
    x_index = lax.axis_index("tp")
    where = jnp.stack([y_index, x_index]).astype(jnp.int32)
    own = jnp.stack([grad, lax.ppermute(grad, "fsdp", Y_SWAP)])
    pieces = [own] + [lax.ppermute(own, "tp", x_shift(s)) for s in range(1, XS)]

    swap = swap_matrix()
    both = jnp.concatenate([first, second], axis=0)
    both = jnp.dot(both, swap, preferred_element_type=jnp.float32).astype(jnp.bfloat16)
    both = both.reshape(2, 192, PLANE, 128).transpose(2, 0, 1, 3)
    moments = plane_exchange(both)

    squares = total_squares(grad)
    limit = clip_ratio * jnp.sqrt(jnp.float32(N * K))
    clip = jnp.minimum(jnp.float32(1.0), limit / jnp.sqrt(squares + 1e-06))

    total = delta.astype(jnp.float32)
    for bit in (1, 2, 3):
        total = total + lax.ppermute(delta, "island", [(i, i ^ bit) for i in range(4)]).astype(jnp.float32)
    delta_mean = total / 4
    momentum = outer_momentum.astype(jnp.float32)
    synced = (row_fragment == sync_fragment[0])[:, None]
    new_momentum = jnp.where(synced, nesterov * momentum + delta_mean, momentum)
    correction = jnp.where(
        synced, outer_rate * (nesterov * new_momentum + delta_mean), jnp.float32(0.0)
    )

    rotated, update = core(where, clip.reshape(1), pieces, basis, moments)
    update = plane_exchange(update)
    rotated = plane_exchange(rotated).transpose(1, 0, 2).reshape(192, 1024)
    rotated = jnp.dot(rotated, swap, preferred_element_type=jnp.float32)
    scaled = clip * rotated
    first_new = beta_first * first.astype(jnp.float32) + (1.0 - beta_first) * scaled
    second_new = beta_second * second.astype(jnp.float32) + (1.0 - beta_second) * scaled * scaled
    update = jnp.sum(update.astype(jnp.float32), axis=0)
    weight_new = weights[0].astype(jnp.float32) - inner_rate * update - correction
    return (
        weight_new.astype(jnp.bfloat16)[None],
        first_new.astype(jnp.bfloat16)[None],
        second_new.astype(jnp.bfloat16)[None],
        new_momentum.astype(jnp.bfloat16),
    )


def solution(mesh):
    in_specs = (
        P("island", "fsdp", "tp"),
        P("island", "fsdp", "tp"),
        P("island", "fsdp", "tp"),
        P("island", "fsdp", "tp"),
        P("island", None, "tp", "fsdp"),
        P("island", "fsdp", "tp"),
        P("fsdp", "tp"),
        P("fsdp"),
        P(),
        P("island"),
    )
    out_specs = (
        P("island", "fsdp", "tp"),
        P("island", "fsdp", "tp"),
        P("island", "fsdp", "tp"),
        P("fsdp", "tp"),
    )
    return jax.shard_map(
        on_device, mesh=mesh, in_specs=in_specs, out_specs=out_specs, check_vma=False
    )
```

```python
import jax
import jax.numpy as jnp
import numpy as np
from jax import lax
from jax.experimental import pallas as pl
from jax.experimental.pallas import tpu as pltpu
from jax.sharding import PartitionSpec as P

K = 4096
N = 6144

beta_first = 0.9
beta_second = 0.95
adam_epsilon = 1e-08
inner_rate = 0.3
outer_rate = 0.7
nesterov = 0.9
clip_ratio = 0.5

ZS = 16
YS = 2
XS = 4
PLANE = YS * XS
BOTH = ("fsdp", "tp")
PLANE_GROUPS = [[(y * ZS + z) * XS + x for y in range(YS) for x in range(XS)] for z in range(ZS)]
Z_GROUPS = [[y * ZS + z for z in range(ZS)] for y in range(YS)]
Y_SWAP = [(f, (f + ZS) % (YS * ZS)) for f in range(YS * ZS)]


def x_shift(s):
    return [(x, (x + s) % XS) for x in range(XS)]


def plane_exchange(value):
    return lax.all_to_all(
        value, BOTH, split_axis=0, concat_axis=0, axis_index_groups=PLANE_GROUPS, tiled=True
    )


def ring_squares(grad):
    total = jnp.full((8, 128), jnp.sum(jnp.square(grad.astype(jnp.float32))))
    for bit in (1, 2, 4, 8):
        total = total + lax.ppermute(total, "fsdp", [(f, f ^ bit) for f in range(YS * ZS)])
    return total[0:1, 0:1]


def three_pieces(value):
    high = lax.reduce_precision(value, 8, 7)
    middle = lax.reduce_precision(value - high, 8, 7)
    low = lax.reduce_precision(value - high - middle, 8, 7)
    rows = jnp.concatenate([high, middle, low, jnp.zeros((13, 1), jnp.float32)], axis=0)
    return jnp.broadcast_to(rows.astype(jnp.bfloat16), (PLANE, 16, 128))


def swap_matrix():
    row = lax.broadcasted_iota(jnp.int32, (1024, 1024), 0)
    col = lax.broadcasted_iota(jnp.int32, (1024, 1024), 1)
    swapped = (col // 16 % 8) * 128 + (col // 128) * 16 + col % 16
    return (row == swapped).astype(jnp.bfloat16)


def core_kernel(where_ref, clip_ref, a0, a1, a2, a3, b_ref, m_ref, out_ref, dir_ref):
    y = where_ref[0]
    x = where_ref[1]
    clip = clip_ref[0]
    acc = jnp.zeros((384, 512), jnp.float32)
    for s, piece in enumerate((a0, a1, a2, a3)):
        at = pl.multiple_of(lax.rem(x + XS - s, XS) * 1024, 1024)
        acc = acc + lax.dot_general(
            piece[...].reshape(384, 1024),
            b_ref[:, pl.ds(at, 1024)],
            (((1,), (1,)), ((), ())),
            preferred_element_type=jnp.float32,
        )
    for u in range(YS):
        row = lax.rem(y + u, YS)
        for t in range(XS):
            rotated = acc[u * 192 : (u + 1) * 192, t * 128 : (t + 1) * 128]
            out_ref[row * XS + t, :, 1024:1152] = rotated.astype(jnp.bfloat16)
            scaled = clip * rotated
            first = m_ref[row * XS + t, 0:192].astype(jnp.float32)
            second = m_ref[row * XS + t, 192:384].astype(jnp.float32)
            first = beta_first * first + (1.0 - beta_first) * scaled
            second = beta_second * second + (1.0 - beta_second) * scaled * scaled
            dir_ref[u * 192 : (u + 1) * 192, t * 128 : (t + 1) * 128] = (
                first / (jnp.sqrt(second) + adam_epsilon)
            ).astype(jnp.bfloat16)
    for t in range(XS):
        update = jnp.dot(
            dir_ref[...], b_ref[:, t * 1024 : (t + 1) * 1024], preferred_element_type=jnp.float32
        ).astype(jnp.bfloat16)
        for u in range(YS):
            out_ref[lax.rem(y + u, YS) * XS + t, :, 0:1024] = update[u * 192 : (u + 1) * 192]


def core(where, clip, pieces, basis, moments):
    vmem = pl.BlockSpec(memory_space=pltpu.VMEM)
    smem = pl.BlockSpec(memory_space=pltpu.SMEM)
    return pl.pallas_call(
        core_kernel,
        out_shape=jax.ShapeDtypeStruct((PLANE, 192, 1152), jnp.bfloat16),
        in_specs=[smem, smem] + [vmem] * 6,
        out_specs=vmem,
        scratch_shapes=[pltpu.VMEM((384, 512), jnp.bfloat16)],
        compiler_params=pltpu.CompilerParams(vmem_limit_bytes=48 * 2**20),
        cost_estimate=pl.CostEstimate(
            flops=4 * 384 * 4096 * 512, bytes_accessed=11 * 2**20, transcendentals=384 * 512
        ),
    )(where, clip, *pieces, basis, moments)


def on_device(
    weights,
    grads,
    first_moment,
    second_moment,
    bases,
    outer_delta,
    outer_momentum,
    row_fragment,
    sync_fragment,
    block_map,
):
    chosen = lax.dynamic_index_in_dim(bases[0], block_map[0], 0, keepdims=False)
    mixed = plane_exchange(chosen.T)
    mixed = mixed.reshape(YS, XS, 16, 1024).transpose(0, 2, 1, 3).reshape(YS, 16, K)
    basis = lax.all_gather(mixed, "fsdp", axis=1, axis_index_groups=Z_GROUPS, tiled=True)
    basis = basis.reshape(512, K)
    mixed, grad = lax.optimization_barrier((mixed, grads[0]))

    y_index = lax.axis_index("fsdp") // ZS
    x_index = lax.axis_index("tp")
    where = jnp.stack([y_index, x_index]).astype(jnp.int32)
    own = jnp.stack([grad, lax.ppermute(grad, "fsdp", Y_SWAP)])
    pieces = [own] + [lax.ppermute(own, "tp", x_shift(s)) for s in range(1, XS)]

    squares = ring_squares(grad)
    squares, first, second, delta = lax.optimization_barrier(
        (squares, first_moment[0], second_moment[0], outer_delta[0])
    )
    swap = swap_matrix()
    both = jnp.concatenate([first, second], axis=0)
    both = jnp.dot(both, swap, preferred_element_type=jnp.float32).astype(jnp.bfloat16)
    both = both.reshape(384, PLANE, 128).transpose(1, 0, 2)
    moments = plane_exchange(jnp.concatenate([both, three_pieces(squares)], axis=1))
    squares = jnp.sum(moments[:, 384:387, 0].astype(jnp.float32))
    limit = clip_ratio * jnp.sqrt(jnp.float32(N * K))
    clip = jnp.minimum(jnp.float32(1.0), limit / jnp.sqrt(squares + 1e-06))

    total = delta.astype(jnp.float32)
    for bit in (1, 2, 3):
        total = total + lax.ppermute(delta, "island", [(i, i ^ bit) for i in range(4)]).astype(jnp.float32)
    delta_mean = total / 4
    momentum = outer_momentum.astype(jnp.float32)
    synced = (row_fragment == sync_fragment[0])[:, None]
    new_momentum = jnp.where(synced, nesterov * momentum + delta_mean, momentum)
    correction = jnp.where(
        synced, outer_rate * (nesterov * new_momentum + delta_mean), jnp.float32(0.0)
    )
    new_momentum = new_momentum.astype(jnp.bfloat16)
    kept = weights[0].astype(jnp.float32) - correction
    kept, new_momentum, moments = lax.optimization_barrier((kept, new_momentum, moments))

    mine = plane_exchange(core(where, clip.reshape(1), pieces, basis, moments))
    rotated = mine[:, :, 1024:].transpose(1, 0, 2).reshape(192, 1024)
    rotated = jnp.dot(rotated, swap, preferred_element_type=jnp.float32)
    scaled = clip * rotated
    first_new = beta_first * first.astype(jnp.float32) + (1.0 - beta_first) * scaled
    second_new = beta_second * second.astype(jnp.float32) + (1.0 - beta_second) * scaled * scaled
    update = jnp.sum(mine[:, :, :1024].astype(jnp.float32), axis=0)
    weight_new = kept - inner_rate * update
    return (
        weight_new.astype(jnp.bfloat16)[None],
        first_new.astype(jnp.bfloat16)[None],
        second_new.astype(jnp.bfloat16)[None],
        new_momentum,
    )


def solution(mesh):
    in_specs = (
        P("island", "fsdp", "tp"),
        P("island", "fsdp", "tp"),
        P("island", "fsdp", "tp"),
        P("island", "fsdp", "tp"),
        P("island", None, "tp", "fsdp"),
        P("island", "fsdp", "tp"),
        P("fsdp", "tp"),
        P("fsdp"),
        P(),
        P("island"),
    )
    out_specs = (
        P("island", "fsdp", "tp"),
        P("island", "fsdp", "tp"),
        P("island", "fsdp", "tp"),
        P("fsdp", "tp"),
    )
    return jax.shard_map(
        on_device, mesh=mesh, in_specs=in_specs, out_specs=out_specs, check_vma=False
    )
```

```python
import jax
import jax.numpy as jnp
import numpy as np
from jax import lax
from jax.experimental import pallas as pl
from jax.experimental.pallas import tpu as pltpu
from jax.sharding import PartitionSpec as P

K = 4096
N = 6144

beta_first = 0.9
beta_second = 0.95
adam_epsilon = 1e-08
inner_rate = 0.3
outer_rate = 0.7
nesterov = 0.9
clip_ratio = 0.5

ZS = 16
YS = 2
XS = 4
PLANE = YS * XS
BOTH = ("fsdp", "tp")
PLANE_GROUPS = [[(y * ZS + z) * XS + x for y in range(YS) for x in range(XS)] for z in range(ZS)]
Z_GROUPS = [[y * ZS + z for z in range(ZS)] for y in range(YS)]


def plane_exchange(value):
    return lax.all_to_all(
        value, BOTH, split_axis=0, concat_axis=0, axis_index_groups=PLANE_GROUPS, tiled=True
    )


def total_squares(grad):
    total = jnp.full((8, 128), jnp.sum(jnp.square(grad.astype(jnp.float32))))
    for bit in (1, 2, 4, 8, 16):
        total = total + lax.ppermute(total, "fsdp", [(f, f ^ bit) for f in range(YS * ZS)])
    for bit in (1, 2):
        total = total + lax.ppermute(total, "tp", [(x, x ^ bit) for x in range(XS)])
    return total[0, 0]


def swap_matrix():
    row = lax.broadcasted_iota(jnp.int32, (1024, 1024), 0)
    col = lax.broadcasted_iota(jnp.int32, (1024, 1024), 1)
    swapped = (col // 16 % 8) * 128 + (col // 128) * 16 + col % 16
    return (row == swapped).astype(jnp.bfloat16)


def core_kernel(clip_ref, b_ref, m_ref, out_ref, dir_ref):
    clip = clip_ref[0]
    acc = jnp.zeros((384, 512), jnp.float32)
    for t in range(XS):
        rows = jnp.concatenate([m_ref[u * XS + t, :, 0:1024] for u in range(YS)], axis=0)
        acc = acc + lax.dot_general(
            rows,
            b_ref[:, t * 1024 : (t + 1) * 1024],
            (((1,), (1,)), ((), ())),
            preferred_element_type=jnp.float32,
        )
    for u in range(YS):
        for t in range(XS):
            rotated = acc[u * 192 : (u + 1) * 192, t * 128 : (t + 1) * 128]
            out_ref[u * XS + t, :, 1024:1152] = rotated.astype(jnp.bfloat16)
            scaled = clip * rotated
            first = m_ref[u * XS + t, :, 1024:1152].astype(jnp.float32)
            second = m_ref[u * XS + t, :, 1152:1280].astype(jnp.float32)
            first = beta_first * first + (1.0 - beta_first) * scaled
            second = beta_second * second + (1.0 - beta_second) * scaled * scaled
            dir_ref[u * 192 : (u + 1) * 192, t * 128 : (t + 1) * 128] = (
                first / (jnp.sqrt(second) + adam_epsilon)
            ).astype(jnp.bfloat16)
    for t in range(XS):
        update = jnp.dot(
            dir_ref[...], b_ref[:, t * 1024 : (t + 1) * 1024], preferred_element_type=jnp.float32
        ).astype(jnp.bfloat16)
        for u in range(YS):
            out_ref[u * XS + t, :, 0:1024] = update[u * 192 : (u + 1) * 192]


def core(clip, basis, arrived):
    vmem = pl.BlockSpec(memory_space=pltpu.VMEM)
    smem = pl.BlockSpec(memory_space=pltpu.SMEM)
    return pl.pallas_call(
        core_kernel,
        out_shape=jax.ShapeDtypeStruct((PLANE, 192, 1152), jnp.bfloat16),
        in_specs=[smem, vmem, vmem],
        out_specs=vmem,
        scratch_shapes=[pltpu.VMEM((384, 512), jnp.bfloat16)],
        compiler_params=pltpu.CompilerParams(vmem_limit_bytes=48 * 2**20),
        cost_estimate=pl.CostEstimate(
            flops=4 * 384 * 4096 * 512, bytes_accessed=11 * 2**20, transcendentals=384 * 512
        ),
    )(clip, basis, arrived)


def on_device(
    weights,
    grads,
    first_moment,
    second_moment,
    bases,
    outer_delta,
    outer_momentum,
    row_fragment,
    sync_fragment,
    block_map,
):
    chosen = lax.dynamic_index_in_dim(bases[0], block_map[0], 0, keepdims=False)
    mixed = plane_exchange(chosen.T)
    mixed = mixed.reshape(YS, XS, 16, 1024).transpose(0, 2, 1, 3).reshape(YS, 16, K)
    basis = lax.all_gather(mixed, "fsdp", axis=1, axis_index_groups=Z_GROUPS, tiled=True)
    basis = basis.reshape(512, K)
    mixed, grad, first, second = lax.optimization_barrier(
        (mixed, grads[0], first_moment[0], second_moment[0])
    )

    swap = swap_matrix()
    both = jnp.concatenate([first, second], axis=0)
    both = jnp.dot(both, swap, preferred_element_type=jnp.float32).astype(jnp.bfloat16)
    both = both.reshape(2, 192, PLANE, 128).transpose(2, 0, 1, 3)
    rows = jnp.broadcast_to(grad, (PLANE, 192, 1024))
    leaving = jnp.concatenate([rows, both[:, 0], both[:, 1]], axis=2)
    leaving, grad, delta = lax.optimization_barrier((leaving, grad, outer_delta[0]))
    arrived = plane_exchange(leaving)
    squares = total_squares(grad)
    limit = clip_ratio * jnp.sqrt(jnp.float32(N * K))
    clip = jnp.minimum(jnp.float32(1.0), limit / jnp.sqrt(squares + 1e-06))

    total = delta.astype(jnp.float32)
    for bit in (1, 2, 3):
        total = total + lax.ppermute(delta, "island", [(i, i ^ bit) for i in range(4)]).astype(jnp.float32)
    delta_mean = total / 4
    momentum = outer_momentum.astype(jnp.float32)
    synced = (row_fragment == sync_fragment[0])[:, None]
    new_momentum = jnp.where(synced, nesterov * momentum + delta_mean, momentum)
    correction = jnp.where(
        synced, outer_rate * (nesterov * new_momentum + delta_mean), jnp.float32(0.0)
    )
    new_momentum = new_momentum.astype(jnp.bfloat16)
    kept = weights[0].astype(jnp.float32) - correction
    kept, new_momentum, clip = lax.optimization_barrier((kept, new_momentum, clip))

    mine = plane_exchange(core(clip.reshape(1), basis, arrived))
    rotated = mine[:, :, 1024:].transpose(1, 0, 2).reshape(192, 1024)
    rotated = jnp.dot(rotated, swap, preferred_element_type=jnp.float32)
    scaled = clip * rotated
    first_new = beta_first * first.astype(jnp.float32) + (1.0 - beta_first) * scaled
    second_new = beta_second * second.astype(jnp.float32) + (1.0 - beta_second) * scaled * scaled
    update = jnp.sum(mine[:, :, :1024].astype(jnp.float32), axis=0)
    weight_new = kept - inner_rate * update
    return (
        weight_new.astype(jnp.bfloat16)[None],
        first_new.astype(jnp.bfloat16)[None],
        second_new.astype(jnp.bfloat16)[None],
        new_momentum,
    )


def solution(mesh):
    in_specs = (
        P("island", "fsdp", "tp"),
        P("island", "fsdp", "tp"),
        P("island", "fsdp", "tp"),
        P("island", "fsdp", "tp"),
        P("island", None, "tp", "fsdp"),
        P("island", "fsdp", "tp"),
        P("fsdp", "tp"),
        P("fsdp"),
        P(),
        P("island"),
    )
    out_specs = (
        P("island", "fsdp", "tp"),
        P("island", "fsdp", "tp"),
        P("island", "fsdp", "tp"),
        P("fsdp", "tp"),
    )
    return jax.shard_map(
        on_device, mesh=mesh, in_specs=in_specs, out_specs=out_specs, check_vma=False
    )
```

```python
import jax
import jax.numpy as jnp
import numpy as np
from jax import lax
from jax.experimental import pallas as pl
from jax.experimental.pallas import tpu as pltpu
from jax.sharding import PartitionSpec as P

K = 4096
N = 6144

beta_first = 0.9
beta_second = 0.95
adam_epsilon = 1e-08
inner_rate = 0.3
outer_rate = 0.7
nesterov = 0.9
clip_ratio = 0.5

ZS = 16
YS = 2
XS = 4
PLANE = YS * XS
BOTH = ("fsdp", "tp")
PLANE_GROUPS = [[(y * ZS + z) * XS + x for y in range(YS) for x in range(XS)] for z in range(ZS)]
Y_GROUPS = [[f, f + ZS] for f in range(ZS)]
Z_GROUPS = [[y * ZS + z for z in range(ZS)] for y in range(YS)]


def plane_exchange(value):
    return lax.all_to_all(
        value, BOTH, split_axis=0, concat_axis=0, axis_index_groups=PLANE_GROUPS, tiled=True
    )


def total_squares(grad):
    total = jnp.full((8, 128), jnp.sum(jnp.square(grad.astype(jnp.float32))))
    for bit in (1, 2, 4, 8):
        total = total + lax.ppermute(total, "fsdp", [(f, f ^ bit) for f in range(YS * ZS)])
    total = lax.psum(lax.psum(total[0, 0], "tp"), "fsdp", axis_index_groups=Y_GROUPS)
    return total


def swap_matrix():
    row = lax.broadcasted_iota(jnp.int32, (1024, 1024), 0)
    col = lax.broadcasted_iota(jnp.int32, (1024, 1024), 1)
    swapped = (col // 16 % 8) * 128 + (col // 128) * 16 + col % 16
    return (row == swapped).astype(jnp.bfloat16)


def core_kernel(clip_ref, b_hbm, m_hbm, out_hbm, b_ref, m_ref, dir_ref, out_ref, b_sem, m_sem, out_sem):
    clip = clip_ref[0]
    b_copies = []
    m_copies = []
    for t in range(XS):
        b_copies.append(
            pltpu.make_async_copy(b_hbm.at[:, pl.ds(t * 1024, 1024)], b_ref.at[t], b_sem.at[t])
        )
        b_copies[t].start()
        for u in range(YS):
            m_copies.append(
                pltpu.make_async_copy(
                    m_hbm.at[u * XS + t], m_ref.at[t, pl.ds(u * 192, 192)], m_sem.at[t * YS + u]
                )
            )
            m_copies[t * YS + u].start()
    acc = jnp.zeros((384, 512), jnp.float32)
    for t in range(XS):
        b_copies[t].wait()
        for u in range(YS):
            m_copies[t * YS + u].wait()
        acc = acc + lax.dot_general(
            m_ref[t, :, 0:1024],
            b_ref[t],
            (((1,), (1,)), ((), ())),
            preferred_element_type=jnp.float32,
        )
    for t in range(XS):
        rotated = acc[:, t * 128 : (t + 1) * 128]
        for u in range(YS):
            out_ref[u * XS + t, :, 1024:1152] = rotated[u * 192 : (u + 1) * 192].astype(jnp.bfloat16)
        scaled = clip * rotated
        first = m_ref[t, :, 1024:1152].astype(jnp.float32)
        second = m_ref[t, :, 1152:1280].astype(jnp.float32)
        first = beta_first * first + (1.0 - beta_first) * scaled
        second = beta_second * second + (1.0 - beta_second) * scaled * scaled
        dir_ref[:, t * 128 : (t + 1) * 128] = (first / (jnp.sqrt(second) + adam_epsilon)).astype(jnp.bfloat16)
    out_copies = []
    for t in range(XS):
        update = jnp.dot(dir_ref[...], b_ref[t], preferred_element_type=jnp.float32).astype(jnp.bfloat16)
        for u in range(YS):
            at = u * XS + t
            out_ref[at, :, 0:1024] = update[u * 192 : (u + 1) * 192]
            out_copies.append(pltpu.make_async_copy(out_ref.at[at], out_hbm.at[at], out_sem.at[at]))
            out_copies[-1].start()
    for copy in out_copies:
        copy.wait()


def core(clip, basis, arrived):
    smem = pl.BlockSpec(memory_space=pltpu.SMEM)
    hbm = pl.BlockSpec(memory_space=pl.ANY)
    return pl.pallas_call(
        core_kernel,
        out_shape=jax.ShapeDtypeStruct((PLANE, 192, 1152), jnp.bfloat16),
        in_specs=[smem, hbm, hbm],
        out_specs=hbm,
        scratch_shapes=[
            pltpu.VMEM((XS, 512, 1024), jnp.bfloat16),
            pltpu.VMEM((XS, 384, 1280), jnp.bfloat16),
            pltpu.VMEM((384, 512), jnp.bfloat16),
            pltpu.VMEM((PLANE, 192, 1152), jnp.bfloat16),
            pltpu.SemaphoreType.DMA((XS,)),
            pltpu.SemaphoreType.DMA((PLANE,)),
            pltpu.SemaphoreType.DMA((PLANE,)),
        ],
        compiler_params=pltpu.CompilerParams(vmem_limit_bytes=48 * 2**20),
        cost_estimate=pl.CostEstimate(
            flops=4 * 384 * 4096 * 512, bytes_accessed=11 * 2**20, transcendentals=384 * 512
        ),
    )(clip, basis, arrived)


def on_device(
    weights,
    grads,
    first_moment,
    second_moment,
    bases,
    outer_delta,
    outer_momentum,
    row_fragment,
    sync_fragment,
    block_map,
):
    chosen = lax.dynamic_index_in_dim(bases[0], block_map[0], 0, keepdims=False)
    mixed = plane_exchange(chosen.T)
    mixed = mixed.reshape(YS, XS, 16, 1024).transpose(0, 2, 1, 3).reshape(YS, 16, K)
    basis = lax.all_gather(mixed, "fsdp", axis=1, axis_index_groups=Z_GROUPS, tiled=True)
    basis = basis.reshape(512, K)
    mixed, grad, first, second = lax.optimization_barrier(
        (mixed, grads[0], first_moment[0], second_moment[0])
    )

    swap = swap_matrix()
    both = jnp.concatenate([first, second], axis=0)
    both = jnp.dot(both, swap, preferred_element_type=jnp.float32).astype(jnp.bfloat16)
    both = both.reshape(2, 192, PLANE, 128).transpose(2, 0, 1, 3)
    rows = jnp.broadcast_to(grad, (PLANE, 192, 1024))
    leaving = jnp.concatenate([rows, both[:, 0], both[:, 1]], axis=2)
    leaving, grad, delta = lax.optimization_barrier((leaving, grad, outer_delta[0]))
    arrived = plane_exchange(leaving)
    squares = total_squares(grad)
    limit = clip_ratio * jnp.sqrt(jnp.float32(N * K))
    clip = jnp.minimum(jnp.float32(1.0), limit / jnp.sqrt(squares + 1e-06))

    total = delta.astype(jnp.float32)
    for bit in (1, 2, 3):
        total = total + lax.ppermute(delta, "island", [(i, i ^ bit) for i in range(4)]).astype(jnp.float32)
    delta_mean = total / 4
    momentum = outer_momentum.astype(jnp.float32)
    synced = (row_fragment == sync_fragment[0])[:, None]
    new_momentum = jnp.where(synced, nesterov * momentum + delta_mean, momentum)
    correction = jnp.where(
        synced, outer_rate * (nesterov * new_momentum + delta_mean), jnp.float32(0.0)
    )
    new_momentum = new_momentum.astype(jnp.bfloat16)
    kept = weights[0].astype(jnp.float32) - correction
    kept, new_momentum, clip = lax.optimization_barrier((kept, new_momentum, clip))

    mine = plane_exchange(core(clip.reshape(1), basis, arrived))
    rotated = mine[:, :, 1024:].transpose(1, 0, 2).reshape(192, 1024)
    rotated = jnp.dot(rotated, swap, preferred_element_type=jnp.float32)
    scaled = clip * rotated
    first_new = beta_first * first.astype(jnp.float32) + (1.0 - beta_first) * scaled
    second_new = beta_second * second.astype(jnp.float32) + (1.0 - beta_second) * scaled * scaled
    update = jnp.sum(mine[:, :, :1024].astype(jnp.float32), axis=0)
    weight_new = kept - inner_rate * update
    return (
        weight_new.astype(jnp.bfloat16)[None],
        first_new.astype(jnp.bfloat16)[None],
        second_new.astype(jnp.bfloat16)[None],
        new_momentum,
    )


def solution(mesh):
    in_specs = (
        P("island", "fsdp", "tp"),
        P("island", "fsdp", "tp"),
        P("island", "fsdp", "tp"),
        P("island", "fsdp", "tp"),
        P("island", None, "tp", "fsdp"),
        P("island", "fsdp", "tp"),
        P("fsdp", "tp"),
        P("fsdp"),
        P(),
        P("island"),
    )
    out_specs = (
        P("island", "fsdp", "tp"),
        P("island", "fsdp", "tp"),
        P("island", "fsdp", "tp"),
        P("fsdp", "tp"),
    )
    return jax.shard_map(
        on_device, mesh=mesh, in_specs=in_specs, out_specs=out_specs, check_vma=False
    )
```

```python
import jax
import jax.numpy as jnp
import numpy as np
from jax import lax
from jax.experimental import pallas as pl
from jax.experimental.pallas import tpu as pltpu
from jax.sharding import PartitionSpec as P

K = 4096
N = 6144

beta_first = 0.9
beta_second = 0.95
adam_epsilon = 1e-08
inner_rate = 0.3
outer_rate = 0.7
nesterov = 0.9
clip_ratio = 0.5

ZS = 16
YS = 2
XS = 4
PLANE = YS * XS
BOTH = ("fsdp", "tp")
PLANE_GROUPS = [[(y * ZS + z) * XS + x for y in range(YS) for x in range(XS)] for z in range(ZS)]
Y_GROUPS = [[f, f + ZS] for f in range(ZS)]
Z_GROUPS = [[y * ZS + z for z in range(ZS)] for y in range(YS)]


def plane_exchange(value):
    return lax.all_to_all(
        value, BOTH, split_axis=0, concat_axis=0, axis_index_groups=PLANE_GROUPS, tiled=True
    )


def total_squares(grad):
    total = jnp.full((8, 128), jnp.sum(jnp.square(grad.astype(jnp.float32))))
    for bit in (1, 2, 4, 8):
        total = total + lax.ppermute(total, "fsdp", [(f, f ^ bit) for f in range(YS * ZS)])
    total = lax.psum(lax.psum(total[0, 0], "tp"), "fsdp", axis_index_groups=Y_GROUPS)
    return total


def swap_matrix():
    row = lax.broadcasted_iota(jnp.int32, (1024, 1024), 0)
    col = lax.broadcasted_iota(jnp.int32, (1024, 1024), 1)
    swapped = (col // 16 % 8) * 128 + (col // 128) * 16 + col % 16
    return (row == swapped).astype(jnp.bfloat16)


def core_kernel(
    clip_ref, b_hbm, m_hbm, out_hbm, b_ref, a_ref, m_ref, dir_ref, out_ref, b_sem, a_sem, m_sem, out_sem
):
    clip = clip_ref[0]
    b_copies = []
    a_copies = []
    m_copies = []
    for t in range(XS):
        lanes = pl.ds(t * 1024, 1024)
        b_copies.append(pltpu.make_async_copy(b_hbm.at[:, lanes], b_ref.at[:, lanes], b_sem.at[t]))
        b_copies[-1].start()
        for u in range(YS):
            at = u * XS + t
            a_copies.append(
                pltpu.make_async_copy(
                    m_hbm.at[at, :, pl.ds(0, 1024)], a_ref.at[pl.ds(u * 192, 192), lanes], a_sem.at[at]
                )
            )
            a_copies[-1].start()
    for t in range(XS):
        for u in range(YS):
            at = u * XS + t
            m_copies.append(
                pltpu.make_async_copy(
                    m_hbm.at[at, :, pl.ds(1024, 256)], m_ref.at[t, pl.ds(u * 192, 192)], m_sem.at[at]
                )
            )
            m_copies[-1].start()
    acc = None
    for t in range(XS):
        b_copies[t].wait()
        for u in range(YS):
            a_copies[t * YS + u].wait()
        part = lax.dot_general(
            a_ref[:, t * 1024 : (t + 1) * 1024],
            b_ref[:, t * 1024 : (t + 1) * 1024],
            (((1,), (1,)), ((), ())),
            preferred_element_type=jnp.float32,
        )
        acc = part if acc is None else acc + part
    for copy in m_copies:
        copy.wait()
    for t in range(XS):
        rotated = acc[:, t * 128 : (t + 1) * 128]
        for u in range(YS):
            out_ref[u * XS + t, :, 1024:1152] = rotated[u * 192 : (u + 1) * 192].astype(jnp.bfloat16)
        scaled = clip * rotated
        first = m_ref[t, :, 0:128].astype(jnp.float32)
        second = m_ref[t, :, 128:256].astype(jnp.float32)
        first = beta_first * first + (1.0 - beta_first) * scaled
        second = beta_second * second + (1.0 - beta_second) * scaled * scaled
        dir_ref[:, t * 128 : (t + 1) * 128] = (first / (jnp.sqrt(second) + adam_epsilon)).astype(jnp.bfloat16)
    out_copies = []
    for t in range(XS):
        update = jnp.dot(
            dir_ref[...], b_ref[:, t * 1024 : (t + 1) * 1024], preferred_element_type=jnp.float32
        ).astype(jnp.bfloat16)
        for u in range(YS):
            at = u * XS + t
            out_ref[at, :, 0:1024] = update[u * 192 : (u + 1) * 192]
            out_copies.append(pltpu.make_async_copy(out_ref.at[at], out_hbm.at[at], out_sem.at[at]))
            out_copies[-1].start()
    for copy in out_copies:
        copy.wait()


def core(clip, basis, arrived):
    smem = pl.BlockSpec(memory_space=pltpu.SMEM)
    hbm = pl.BlockSpec(memory_space=pl.ANY)
    return pl.pallas_call(
        core_kernel,
        out_shape=jax.ShapeDtypeStruct((PLANE, 192, 1152), jnp.bfloat16),
        in_specs=[smem, hbm, hbm],
        out_specs=hbm,
        scratch_shapes=[
            pltpu.VMEM((512, K), jnp.bfloat16),
            pltpu.VMEM((384, K), jnp.bfloat16),
            pltpu.VMEM((XS, 384, 256), jnp.bfloat16),
            pltpu.VMEM((384, 512), jnp.bfloat16),
            pltpu.VMEM((PLANE, 192, 1152), jnp.bfloat16),
            pltpu.SemaphoreType.DMA((XS,)),
            pltpu.SemaphoreType.DMA((PLANE,)),
            pltpu.SemaphoreType.DMA((PLANE,)),
            pltpu.SemaphoreType.DMA((PLANE,)),
        ],
        compiler_params=pltpu.CompilerParams(vmem_limit_bytes=48 * 2**20),
        cost_estimate=pl.CostEstimate(
            flops=4 * 384 * 4096 * 512, bytes_accessed=11 * 2**20, transcendentals=384 * 512
        ),
    )(clip, basis, arrived)


def on_device(
    weights,
    grads,
    first_moment,
    second_moment,
    bases,
    outer_delta,
    outer_momentum,
    row_fragment,
    sync_fragment,
    block_map,
):
    chosen = lax.dynamic_index_in_dim(bases[0], block_map[0], 0, keepdims=False)
    mixed = plane_exchange(chosen.T)
    mixed = mixed.reshape(YS, XS, 16, 1024).transpose(0, 2, 1, 3).reshape(YS, 16, K)
    basis = lax.all_gather(mixed, "fsdp", axis=1, axis_index_groups=Z_GROUPS, tiled=True)
    basis = basis.reshape(512, K)
    mixed, grad, first, second = lax.optimization_barrier(
        (mixed, grads[0], first_moment[0], second_moment[0])
    )

    swap = swap_matrix()
    both = jnp.concatenate([first, second], axis=0)
    both = jnp.dot(both, swap, preferred_element_type=jnp.float32).astype(jnp.bfloat16)
    both = both.reshape(2, 192, PLANE, 128).transpose(2, 0, 1, 3)
    rows = jnp.broadcast_to(grad, (PLANE, 192, 1024))
    leaving = jnp.concatenate([rows, both[:, 0], both[:, 1]], axis=2)
    leaving, grad, delta = lax.optimization_barrier((leaving, grad, outer_delta[0]))
    arrived = plane_exchange(leaving)
    squares = total_squares(grad)
    limit = clip_ratio * jnp.sqrt(jnp.float32(N * K))
    clip = jnp.minimum(jnp.float32(1.0), limit / jnp.sqrt(squares + 1e-06))

    total = delta.astype(jnp.float32)
    for bit in (1, 2, 3):
        total = total + lax.ppermute(delta, "island", [(i, i ^ bit) for i in range(4)]).astype(jnp.float32)
    delta_mean = total / 4
    momentum = outer_momentum.astype(jnp.float32)
    synced = (row_fragment == sync_fragment[0])[:, None]
    new_momentum = jnp.where(synced, nesterov * momentum + delta_mean, momentum)
    correction = jnp.where(
        synced, outer_rate * (nesterov * new_momentum + delta_mean), jnp.float32(0.0)
    )
    new_momentum = new_momentum.astype(jnp.bfloat16)
    kept = weights[0].astype(jnp.float32) - correction
    kept, new_momentum, clip = lax.optimization_barrier((kept, new_momentum, clip))

    mine = plane_exchange(core(clip.reshape(1), basis, arrived))
    rotated = mine[:, :, 1024:].transpose(1, 0, 2).reshape(192, 1024)
    rotated = jnp.dot(rotated, swap, preferred_element_type=jnp.float32)
    scaled = clip * rotated
    first_new = beta_first * first.astype(jnp.float32) + (1.0 - beta_first) * scaled
    second_new = beta_second * second.astype(jnp.float32) + (1.0 - beta_second) * scaled * scaled
    update = jnp.sum(mine[:, :, :1024].astype(jnp.float32), axis=0)
    weight_new = kept - inner_rate * update
    return (
        weight_new.astype(jnp.bfloat16)[None],
        first_new.astype(jnp.bfloat16)[None],
        second_new.astype(jnp.bfloat16)[None],
        new_momentum,
    )


def solution(mesh):
    in_specs = (
        P("island", "fsdp", "tp"),
        P("island", "fsdp", "tp"),
        P("island", "fsdp", "tp"),
        P("island", "fsdp", "tp"),
        P("island", None, "tp", "fsdp"),
        P("island", "fsdp", "tp"),
        P("fsdp", "tp"),
        P("fsdp"),
        P(),
        P("island"),
    )
    out_specs = (
        P("island", "fsdp", "tp"),
        P("island", "fsdp", "tp"),
        P("island", "fsdp", "tp"),
        P("fsdp", "tp"),
    )
    return jax.shard_map(
        on_device, mesh=mesh, in_specs=in_specs, out_specs=out_specs, check_vma=False
    )
```

```python
import jax
import jax.numpy as jnp
import numpy as np
from jax import lax
from jax.experimental import pallas as pl
from jax.experimental.pallas import tpu as pltpu
from jax.sharding import PartitionSpec as P

K = 4096
N = 6144

beta_first = 0.9
beta_second = 0.95
adam_epsilon = 1e-08
inner_rate = 0.3
outer_rate = 0.7
nesterov = 0.9
clip_ratio = 0.5

ZS = 16
YS = 2
XS = 4
PLANE = YS * XS
BOTH = ("fsdp", "tp")
PLANE_GROUPS = [[(y * ZS + z) * XS + x for y in range(YS) for x in range(XS)] for z in range(ZS)]
Y_GROUPS = [[f, f + ZS] for f in range(ZS)]
Z_GROUPS = [[y * ZS + z for z in range(ZS)] for y in range(YS)]


def plane_exchange(value):
    return lax.all_to_all(
        value, BOTH, split_axis=0, concat_axis=0, axis_index_groups=PLANE_GROUPS, tiled=True
    )


def total_squares(grad):
    total = jnp.full((8, 128), jnp.sum(jnp.square(grad.astype(jnp.float32))))
    for bit in (1, 2, 4, 8):
        total = total + lax.ppermute(total, "fsdp", [(f, f ^ bit) for f in range(YS * ZS)])
    total = lax.psum(lax.psum(total[0, 0], "tp"), "fsdp", axis_index_groups=Y_GROUPS)
    return total


def swap_matrix():
    row = lax.broadcasted_iota(jnp.int32, (1024, 1024), 0)
    col = lax.broadcasted_iota(jnp.int32, (1024, 1024), 1)
    swapped = (col // 16 % 8) * 128 + (col // 128) * 16 + col % 16
    return (row == swapped).astype(jnp.bfloat16)


def core_kernel(
    clip_ref, b_hbm, m_hbm, out_hbm, b_ref, a_ref, m_ref, dir_ref, out_ref, b_sem, a_sem, m_sem, out_sem
):
    clip = clip_ref[0]
    b_copies = []
    a_copies = []
    m_copies = []
    for t in range(XS):
        lanes = pl.ds(t * 1024, 1024)
        for u in range(YS):
            at = u * XS + t
            b_copies.append(
                pltpu.make_async_copy(b_hbm.at[:, at], b_ref.at[u, :, :, lanes], b_sem.at[at])
            )
            b_copies[-1].start()
            a_copies.append(
                pltpu.make_async_copy(
                    m_hbm.at[at, :, pl.ds(0, 1024)], a_ref.at[pl.ds(u * 192, 192), lanes], a_sem.at[at]
                )
            )
            a_copies[-1].start()
    for t in range(XS):
        for u in range(YS):
            at = u * XS + t
            m_copies.append(
                pltpu.make_async_copy(
                    m_hbm.at[at, :, pl.ds(1024, 256)], m_ref.at[t, pl.ds(u * 192, 192)], m_sem.at[at]
                )
            )
            m_copies[-1].start()
    acc = None
    for t in range(XS):
        for u in range(YS):
            b_copies[t * YS + u].wait()
            a_copies[t * YS + u].wait()
        part = lax.dot_general(
            a_ref[:, t * 1024 : (t + 1) * 1024],
            b_ref[:, :, :, t * 1024 : (t + 1) * 1024].reshape(512, 1024),
            (((1,), (1,)), ((), ())),
            preferred_element_type=jnp.float32,
        )
        acc = part if acc is None else acc + part
    for copy in m_copies:
        copy.wait()
    for t in range(XS):
        rotated = acc[:, t * 128 : (t + 1) * 128]
        for u in range(YS):
            out_ref[u * XS + t, :, 1024:1152] = rotated[u * 192 : (u + 1) * 192].astype(jnp.bfloat16)
        scaled = clip * rotated
        first = m_ref[t, :, 0:128].astype(jnp.float32)
        second = m_ref[t, :, 128:256].astype(jnp.float32)
        first = beta_first * first + (1.0 - beta_first) * scaled
        second = beta_second * second + (1.0 - beta_second) * scaled * scaled
        dir_ref[:, t * 128 : (t + 1) * 128] = (first / (jnp.sqrt(second) + adam_epsilon)).astype(jnp.bfloat16)
    out_copies = []
    for t in range(XS):
        update = jnp.dot(
            dir_ref[...],
            b_ref[:, :, :, t * 1024 : (t + 1) * 1024].reshape(512, 1024),
            preferred_element_type=jnp.float32
        ).astype(jnp.bfloat16)
        for u in range(YS):
            at = u * XS + t
            out_ref[at, :, 0:1024] = update[u * 192 : (u + 1) * 192]
            out_copies.append(pltpu.make_async_copy(out_ref.at[at], out_hbm.at[at], out_sem.at[at]))
            out_copies[-1].start()
    for copy in out_copies:
        copy.wait()


def core(clip, basis, arrived):
    smem = pl.BlockSpec(memory_space=pltpu.SMEM)
    hbm = pl.BlockSpec(memory_space=pl.ANY)
    return pl.pallas_call(
        core_kernel,
        out_shape=jax.ShapeDtypeStruct((PLANE, 192, 1152), jnp.bfloat16),
        in_specs=[smem, hbm, hbm],
        out_specs=hbm,
        scratch_shapes=[
            pltpu.VMEM((YS, ZS, 16, K), jnp.bfloat16),
            pltpu.VMEM((384, K), jnp.bfloat16),
            pltpu.VMEM((XS, 384, 256), jnp.bfloat16),
            pltpu.VMEM((384, 512), jnp.bfloat16),
            pltpu.VMEM((PLANE, 192, 1152), jnp.bfloat16),
            pltpu.SemaphoreType.DMA((PLANE,)),
            pltpu.SemaphoreType.DMA((PLANE,)),
            pltpu.SemaphoreType.DMA((PLANE,)),
            pltpu.SemaphoreType.DMA((PLANE,)),
        ],
        compiler_params=pltpu.CompilerParams(vmem_limit_bytes=48 * 2**20),
        cost_estimate=pl.CostEstimate(
            flops=4 * 384 * 4096 * 512, bytes_accessed=11 * 2**20, transcendentals=384 * 512
        ),
    )(clip, basis, arrived)


def on_device(
    weights,
    grads,
    first_moment,
    second_moment,
    bases,
    outer_delta,
    outer_momentum,
    row_fragment,
    sync_fragment,
    block_map,
):
    chosen = lax.dynamic_index_in_dim(bases[0], block_map[0], 0, keepdims=False)
    mixed = plane_exchange(chosen.T)
    basis = lax.all_gather(mixed, "fsdp", axis=0, axis_index_groups=Z_GROUPS, tiled=True)
    basis = basis.reshape(ZS, PLANE, 16, 1024)
    mixed, grad, first, second = lax.optimization_barrier(
        (mixed, grads[0], first_moment[0], second_moment[0])
    )

    swap = swap_matrix()
    both = jnp.concatenate([first, second], axis=0)
    both = jnp.dot(both, swap, preferred_element_type=jnp.float32).astype(jnp.bfloat16)
    both = both.reshape(2, 192, PLANE, 128).transpose(2, 0, 1, 3)
    rows = jnp.broadcast_to(grad, (PLANE, 192, 1024))
    leaving = jnp.concatenate([rows, both[:, 0], both[:, 1]], axis=2)
    leaving, grad, delta = lax.optimization_barrier((leaving, grad, outer_delta[0]))
    arrived = plane_exchange(leaving)
    squares = total_squares(grad)
    limit = clip_ratio * jnp.sqrt(jnp.float32(N * K))
    clip = jnp.minimum(jnp.float32(1.0), limit / jnp.sqrt(squares + 1e-06))

    total = delta.astype(jnp.float32)
    for bit in (1, 2, 3):
        total = total + lax.ppermute(delta, "island", [(i, i ^ bit) for i in range(4)]).astype(jnp.float32)
    delta_mean = total / 4
    momentum = outer_momentum.astype(jnp.float32)
    synced = (row_fragment == sync_fragment[0])[:, None]
    new_momentum = jnp.where(synced, nesterov * momentum + delta_mean, momentum)
    correction = jnp.where(
        synced, outer_rate * (nesterov * new_momentum + delta_mean), jnp.float32(0.0)
    )
    new_momentum = new_momentum.astype(jnp.bfloat16)
    kept = weights[0].astype(jnp.float32) - correction
    kept, new_momentum, clip = lax.optimization_barrier((kept, new_momentum, clip))

    mine = plane_exchange(core(clip.reshape(1), basis, arrived))
    rotated = mine[:, :, 1024:].transpose(1, 0, 2).reshape(192, 1024)
    rotated = jnp.dot(rotated, swap, preferred_element_type=jnp.float32)
    scaled = clip * rotated
    first_new = beta_first * first.astype(jnp.float32) + (1.0 - beta_first) * scaled
    second_new = beta_second * second.astype(jnp.float32) + (1.0 - beta_second) * scaled * scaled
    update = jnp.sum(mine[:, :, :1024].astype(jnp.float32), axis=0)
    weight_new = kept - inner_rate * update
    return (
        weight_new.astype(jnp.bfloat16)[None],
        first_new.astype(jnp.bfloat16)[None],
        second_new.astype(jnp.bfloat16)[None],
        new_momentum,
    )


def solution(mesh):
    in_specs = (
        P("island", "fsdp", "tp"),
        P("island", "fsdp", "tp"),
        P("island", "fsdp", "tp"),
        P("island", "fsdp", "tp"),
        P("island", None, "tp", "fsdp"),
        P("island", "fsdp", "tp"),
        P("fsdp", "tp"),
        P("fsdp"),
        P(),
        P("island"),
    )
    out_specs = (
        P("island", "fsdp", "tp"),
        P("island", "fsdp", "tp"),
        P("island", "fsdp", "tp"),
        P("fsdp", "tp"),
    )
    return jax.shard_map(
        on_device, mesh=mesh, in_specs=in_specs, out_specs=out_specs, check_vma=False
    )
```

```python
import jax
import jax.numpy as jnp
import numpy as np
from jax import lax
from jax.experimental import pallas as pl
from jax.experimental.pallas import tpu as pltpu
from jax.sharding import PartitionSpec as P

K = 4096
N = 6144

beta_first = 0.9
beta_second = 0.95
adam_epsilon = 1e-08
inner_rate = 0.3
outer_rate = 0.7
nesterov = 0.9
clip_ratio = 0.5

ZS = 16
YS = 2
XS = 4
PLANE = YS * XS
BOTH = ("fsdp", "tp")
PLANE_GROUPS = [[(y * ZS + z) * XS + x for y in range(YS) for x in range(XS)] for z in range(ZS)]
Y_GROUPS = [[f, f + ZS] for f in range(ZS)]
Z_GROUPS = [[y * ZS + z for z in range(ZS)] for y in range(YS)]


def plane_exchange(value):
    return lax.all_to_all(
        value, BOTH, split_axis=0, concat_axis=0, axis_index_groups=PLANE_GROUPS, tiled=True
    )


def total_squares(grad):
    total = jnp.full((8, 128), jnp.sum(jnp.square(grad.astype(jnp.float32))))
    for bit in (1, 2, 4, 8):
        total = total + lax.ppermute(total, "fsdp", [(f, f ^ bit) for f in range(YS * ZS)])
    total = lax.psum(lax.psum(total[0, 0], "tp"), "fsdp", axis_index_groups=Y_GROUPS)
    return total


def swap_matrix():
    row = lax.broadcasted_iota(jnp.int32, (1024, 1024), 0)
    col = lax.broadcasted_iota(jnp.int32, (1024, 1024), 1)
    swapped = (col // 16 % 8) * 128 + (col // 128) * 16 + col % 16
    return (row == swapped).astype(jnp.bfloat16)


def core_kernel(
    clip_ref, b_hbm, m_hbm, out_hbm, b_ref, a_ref, m_ref, dir_ref, out_ref, b_sem, a_sem, m_sem, out_sem
):
    clip = clip_ref[0]
    b_copies = []
    a_copies = []
    m_copies = []
    for t in range(XS):
        lanes = pl.ds(t * 1024, 1024)
        for u in range(YS):
            at = u * XS + t
            b_copies.append(
                pltpu.make_async_copy(b_hbm.at[:, at], b_ref.at[u, :, :, lanes], b_sem.at[at])
            )
            b_copies[-1].start()
            a_copies.append(
                pltpu.make_async_copy(
                    m_hbm.at[at, :, pl.ds(0, 1024)], a_ref.at[pl.ds(u * 192, 192), lanes], a_sem.at[at]
                )
            )
            a_copies[-1].start()
    for t in range(XS):
        for u in range(YS):
            at = u * XS + t
            m_copies.append(
                pltpu.make_async_copy(
                    m_hbm.at[at, :, pl.ds(1024, 256)], m_ref.at[t, pl.ds(u * 192, 192)], m_sem.at[at]
                )
            )
            m_copies[-1].start()
    acc = None
    for t in range(XS):
        for u in range(YS):
            b_copies[t * YS + u].wait()
            a_copies[t * YS + u].wait()
        part = lax.dot_general(
            a_ref[:, t * 1024 : (t + 1) * 1024],
            b_ref[:, :, :, t * 1024 : (t + 1) * 1024].reshape(512, 1024),
            (((1,), (1,)), ((), ())),
            preferred_element_type=jnp.float32,
        )
        acc = part if acc is None else acc + part
    for copy in m_copies:
        copy.wait()
    for t in range(XS):
        rotated = acc[:, t * 128 : (t + 1) * 128]
        for u in range(YS):
            out_ref[u * XS + t, :, 1024:1152] = rotated[u * 192 : (u + 1) * 192].astype(jnp.bfloat16)
        scaled = clip * rotated
        first = m_ref[t, :, 0:128].astype(jnp.float32)
        second = m_ref[t, :, 128:256].astype(jnp.float32)
        first = beta_first * first + (1.0 - beta_first) * scaled
        second = beta_second * second + (1.0 - beta_second) * scaled * scaled
        dir_ref[:, t * 128 : (t + 1) * 128] = (first / (jnp.sqrt(second) + adam_epsilon)).astype(jnp.bfloat16)
    out_copies = []
    for t in range(XS):
        update = jnp.dot(
            dir_ref[...],
            b_ref[:, :, :, t * 1024 : (t + 1) * 1024].reshape(512, 1024),
            preferred_element_type=jnp.float32
        ).astype(jnp.bfloat16)
        for u in range(YS):
            at = u * XS + t
            out_ref[at, :, 0:1024] = update[u * 192 : (u + 1) * 192]
            out_copies.append(pltpu.make_async_copy(out_ref.at[at], out_hbm.at[at], out_sem.at[at]))
            out_copies[-1].start()
    for copy in out_copies:
        copy.wait()


def core(clip, basis, arrived):
    smem = pl.BlockSpec(memory_space=pltpu.SMEM)
    hbm = pl.BlockSpec(memory_space=pl.ANY)
    return pl.pallas_call(
        core_kernel,
        out_shape=jax.ShapeDtypeStruct((PLANE, 192, 1152), jnp.bfloat16),
        in_specs=[smem, hbm, hbm],
        out_specs=hbm,
        scratch_shapes=[
            pltpu.VMEM((YS, ZS, 16, K), jnp.bfloat16),
            pltpu.VMEM((384, K), jnp.bfloat16),
            pltpu.VMEM((XS, 384, 256), jnp.bfloat16),
            pltpu.VMEM((384, 512), jnp.bfloat16),
            pltpu.VMEM((PLANE, 192, 1152), jnp.bfloat16),
            pltpu.SemaphoreType.DMA((PLANE,)),
            pltpu.SemaphoreType.DMA((PLANE,)),
            pltpu.SemaphoreType.DMA((PLANE,)),
            pltpu.SemaphoreType.DMA((PLANE,)),
        ],
        compiler_params=pltpu.CompilerParams(vmem_limit_bytes=24 * 2**20),
        cost_estimate=pl.CostEstimate(
            flops=4 * 384 * 4096 * 512, bytes_accessed=11 * 2**20, transcendentals=384 * 512
        ),
    )(clip, basis, arrived)


def on_device(
    weights,
    grads,
    first_moment,
    second_moment,
    bases,
    outer_delta,
    outer_momentum,
    row_fragment,
    sync_fragment,
    block_map,
):
    chosen = lax.dynamic_index_in_dim(bases[0], block_map[0], 0, keepdims=False)
    mixed = plane_exchange(chosen.T)
    basis = lax.all_gather(mixed, "fsdp", axis=0, axis_index_groups=Z_GROUPS, tiled=True)
    basis = basis.reshape(ZS, PLANE, 16, 1024)
    mixed, grad, first, second = lax.optimization_barrier(
        (mixed, grads[0], first_moment[0], second_moment[0])
    )

    swap = swap_matrix()
    both = jnp.concatenate([first, second], axis=0)
    both = jnp.dot(both, swap, preferred_element_type=jnp.float32).astype(jnp.bfloat16)
    both = both.reshape(2, 192, PLANE, 128).transpose(2, 0, 1, 3)
    rows = jnp.broadcast_to(grad, (PLANE, 192, 1024))
    leaving = jnp.concatenate([rows, both[:, 0], both[:, 1]], axis=2)
    leaving, grad, delta = lax.optimization_barrier((leaving, grad, outer_delta[0]))
    arrived = plane_exchange(leaving)
    squares = total_squares(grad)
    limit = clip_ratio * jnp.sqrt(jnp.float32(N * K))
    clip = jnp.minimum(jnp.float32(1.0), limit / jnp.sqrt(squares + 1e-06))

    total = delta.astype(jnp.float32)
    for bit in (1, 2, 3):
        total = total + lax.ppermute(delta, "island", [(i, i ^ bit) for i in range(4)]).astype(jnp.float32)
    delta_mean = total / 4
    momentum = outer_momentum.astype(jnp.float32)
    synced = (row_fragment == sync_fragment[0])[:, None]
    new_momentum = jnp.where(synced, nesterov * momentum + delta_mean, momentum)
    correction = jnp.where(
        synced, outer_rate * (nesterov * new_momentum + delta_mean), jnp.float32(0.0)
    )
    new_momentum = new_momentum.astype(jnp.bfloat16)
    kept = weights[0].astype(jnp.float32) - correction
    kept, new_momentum, clip = lax.optimization_barrier((kept, new_momentum, clip))

    mine = plane_exchange(core(clip.reshape(1), basis, arrived))
    rotated = mine[:, :, 1024:].transpose(1, 0, 2).reshape(192, 1024)
    rotated = jnp.dot(rotated, swap, preferred_element_type=jnp.float32)
    scaled = clip * rotated
    first_new = beta_first * first.astype(jnp.float32) + (1.0 - beta_first) * scaled
    second_new = beta_second * second.astype(jnp.float32) + (1.0 - beta_second) * scaled * scaled
    update = jnp.sum(mine[:, :, :1024].astype(jnp.float32), axis=0)
    weight_new = kept - inner_rate * update
    return (
        weight_new.astype(jnp.bfloat16)[None],
        first_new.astype(jnp.bfloat16)[None],
        second_new.astype(jnp.bfloat16)[None],
        new_momentum,
    )


def solution(mesh):
    in_specs = (
        P("island", "fsdp", "tp"),
        P("island", "fsdp", "tp"),
        P("island", "fsdp", "tp"),
        P("island", "fsdp", "tp"),
        P("island", None, "tp", "fsdp"),
        P("island", "fsdp", "tp"),
        P("fsdp", "tp"),
        P("fsdp"),
        P(),
        P("island"),
    )
    out_specs = (
        P("island", "fsdp", "tp"),
        P("island", "fsdp", "tp"),
        P("island", "fsdp", "tp"),
        P("fsdp", "tp"),
    )
    return jax.shard_map(
        on_device, mesh=mesh, in_specs=in_specs, out_specs=out_specs, check_vma=False
    )
```
